512 devices in a mesh: wide: 64 (over x, y, core), narrow: 8 (over z).
Axes of the slice: x: 4, y: 8, z: 8, core: 2. Of those that a mesh axis runs over, the one named last changes fastest.
Arguments:
- amplitudes: bfloat16 [3, 3072, 3072], P(None, 'wide', 'narrow'), may hold values from -6 to 6
- crossed: bfloat16 [3, 3072, 3072], P(None, 'wide', 'narrow'), may hold values from -6 to 6
- coulomb: bfloat16 [3, 3072, 3072], P(None, 'wide', 'narrow'), may hold values from -0.109375 to 0.109375
- exchange_int: bfloat16 [3, 3072, 3072], P(None, 'wide', 'narrow'), may hold values from -0.109375 to 0.109375
- block_order: int32 [3], replicated, may hold values from 1 to 3072, 6912 in all
Outputs:
- residual: bfloat16 [3, 3072, 3072], P(None, 'wide', 'narrow')
The draws below stay inside these ranges and needn't reach their ends.
Inputs may be any that keep to these rules, and one draw needn't show every extreme that they name: `block_order`: the entries sum to 6912 and the largest is exactly 3072.
All inputs are finite; a program needn't handle non-finite values.
Results may differ from the reference program's by a relative error of at most 0.017.
Values may be sent and summed in bfloat16 or wider, within the bound.
No kernel may reach another device: no remote copies, remote signals or barrier semaphores. Data moves between devices by JAX's collectives and lax.ppermute only.
A program may use at most 128 MiB of HBM per device.

```python
import math
import jax
import jax.numpy as jnp
import numpy as np
from jax import lax

NB = 3
S = 3072
LAYERS = 8


def block_levels(own_key, dims, cuts, least, high):
    def one(dim, blocks):
        steps = jax.random.uniform(jax.random.fold_in(jax.random.fold_in(own_key, 6), dim), (blocks,), jnp.float32, least / len(cuts), high / len(cuts))
        return jnp.repeat(jnp.exp(steps), dims[dim] // blocks).reshape((-1,) + (1,) * (len(dims) - dim - 1))

    level = one(*cuts[0])
    for cut in cuts[1:]:
        level = level * one(*cut)
    return level


def length_profile(amount, total, bound, lean):
    loads = [(1 << 20) // math.isqrt(rank ** lean) + 1 for rank in range(2, amount + 1)]
    surplus, holding = total - bound - (amount - 1), [1] * (amount - 1)
    while surplus > 0:
        candidates = [i for i in range(amount - 1) if holding[i] < bound]
        whole, budget = sum([loads[i] for i in candidates]), surplus
        for i in candidates:
            more = min(bound - holding[i], max(1, budget * loads[i] // whole), surplus)
            holding[i] = holding[i] + more
            surplus = surplus - more
    return np.array([bound] + holding)


def ragged(key, amount, total, limit, skew):
    if amount == 2:
        one = jax.random.randint(key, (), max(1, total - limit), min(limit, total - 1) + 1)
        return jnp.stack([one, total - one])
    tallies = jnp.asarray(length_profile(amount, total, limit, skew), jnp.int32)
    twos = (amount - 1) // 2
    donor, taker = tallies[1:1 + 2 * twos:2], tallies[2:2 + 2 * twos:2]
    slack = jnp.minimum(donor - 1, limit - taker)
    moved = jax.random.randint(jax.random.fold_in(key, 1), (twos,), 0, 1 << 20) % (slack + 1)
    tallies = tallies.at[1:1 + 2 * twos:2].set(donor - moved).at[2:2 + 2 * twos:2].set(taker + moved)
    return tallies[jax.random.permutation(jax.random.fold_in(key, 2), amount)]


def noise(own_key, shape, spread, most, shards=(), kind=jnp.bfloat16):
    factor_of = block_levels(own_key, shape, shards, -0.22, 0.18) if shards else 1.0
    result = jax.random.normal(own_key, shape, jnp.float32) * spread * factor_of
    return jnp.minimum(jnp.maximum(result, -most), most).astype(kind)


def setup_inputs(seed: int = 0) -> dict:
    keys = jax.random.split(jax.random.key(seed), 6)
    return {
        "amplitudes": noise(keys[0], (NB, S, S), 1.0, 6.0, ((1, 64), (2, 8))),
        "crossed": noise(keys[1], (NB, S, S), 1.0, 6.0, ((1, 64), (2, 8))),
        "coulomb": noise(keys[2], (NB, S, S), S ** -0.5, 0.109375, ((1, 64), (2, 8))),
        "exchange_int": noise(keys[3], (NB, S, S), S ** -0.5, 0.109375, ((1, 64), (2, 8))),
        "block_order": ragged(keys[4], NB, NB * S * 3 // 4, S, 0).astype(jnp.int32),
    }


def one_block(pieces):
    amplitudes, crossed, coulomb, exchange_int, length = pieces
    positions = jnp.arange(S, dtype=jnp.int32)
    live_half = (positions < length).astype(jnp.bfloat16)
    masked_amp = amplitudes * live_half[None, :]
    masked_cross = crossed * live_half[None, :]
    layer_width = S // LAYERS
    summed = jnp.zeros((S, S), jnp.float32)
    for which_layer in range(LAYERS):
        offset = which_layer * layer_width
        product = jnp.dot(masked_amp[:, offset:offset + layer_width], coulomb[:, offset:offset + layer_width].T, preferred_element_type=jnp.float32)
        product = product + jnp.dot(masked_cross[:, offset:offset + layer_width], exchange_int[:, offset:offset + layer_width].T, preferred_element_type=jnp.float32)
        rounded = lax.optimization_barrier(product.astype(jnp.bfloat16))
        summed = summed + rounded.astype(jnp.float32)
    live_mask = (positions < length).astype(jnp.float32)
    return (summed * live_mask[:, None] * live_mask[None, :]).astype(jnp.bfloat16)


def reference(amplitudes, crossed, coulomb, exchange_int, block_order):
    return lax.map(one_block, (amplitudes, crossed, coulomb, exchange_int, block_order))
```

```python
import jax
import jax.numpy as jnp
from jax import lax
from jax.experimental import pallas as pl
from jax.experimental.pallas import tpu as pltpu
from jax.sharding import Mesh, PartitionSpec as P

NX, NY, NC, NZ = 4, 8, 2, 8
NH, ROWS, DEPTH = 3, 48, 384


def tile_kernel(order_ref, left_ref, right_ref, out_ref, *, col_tile):
    x, y, c, z = (order_ref[NH + i] for i in range(4))
    col = lax.broadcasted_iota(jnp.int32, (1, DEPTH), 1)
    for h in range(NH):
        length = order_ref[h]
        live_k = (z * DEPTH + col) < length
        total = None
        for pair in range(2):
            left = left_ref[:, pair, h].reshape(NX * ROWS, DEPTH)
            left = jnp.where(live_k, left, jnp.zeros_like(left))
            right = right_ref[:, pair, h].reshape(NY * NC * ROWS, DEPTH)
            part = lax.dot_general(
                left, right, (((1,), (1,)), ((), ())), preferred_element_type=jnp.float32
            )
            total = part if total is None else total + part
        for xx in range(NX):
            row = lax.broadcasted_iota(jnp.int32, (ROWS, 1), 0)
            row = ((xx * NY + y) * NC + c) * ROWS + row
            for half in range(2):
                b = (x * 2 + half) * col_tile + col
                live = (row < length) & (b < length)
                block = total[xx * ROWS : (xx + 1) * ROWS, half * col_tile : (half + 1) * col_tile]
                out_ref[xx * 2 + half, h] = jnp.where(live, block, 0.0).astype(jnp.bfloat16)


def local(amplitudes, crossed, coulomb, exchange_int, block_order):
    x, y, c, z = (lax.axis_index(n) for n in ("x", "y", "c", "z"))
    place = jnp.concatenate([block_order, jnp.stack([x, y, c, z]).astype(jnp.int32)])
    left = lax.all_gather(jnp.stack([amplitudes, crossed]), "x")
    right = lax.all_gather(jnp.stack([coulomb, exchange_int]), ("y", "c"))
    col_tile = NY * NC * ROWS // 2
    pieces = pl.pallas_call(
        lambda *refs: tile_kernel(*refs, col_tile=col_tile),
        out_shape=jax.ShapeDtypeStruct((NX * 2, NH, ROWS, col_tile), jnp.bfloat16),
        in_specs=[
            pl.BlockSpec(memory_space=pltpu.SMEM),
            pl.BlockSpec(memory_space=pltpu.VMEM),
            pl.BlockSpec(memory_space=pltpu.VMEM),
        ],
        out_specs=pl.BlockSpec(memory_space=pltpu.VMEM),
        compiler_params=pltpu.CompilerParams(vmem_limit_bytes=32 * 2**20),
    )(place, left, right)
    summed = lax.psum_scatter(pieces, "z", scatter_dimension=0)
    moves = [
        (xs * NZ + xd * 2 + half, xd * NZ + xs * 2 + half)
        for xs in range(NX)
        for xd in range(NX)
        for half in range(2)
    ]
    return lax.ppermute(summed, ("x", "z"), moves)


def solution(mesh):
    grid = Mesh(mesh.devices.reshape(NX, NY, NC, NZ), ("x", "y", "c", "z"))
    spec = P(None, ("x", "y", "c"), "z")
    return jax.shard_map(
        local, mesh=grid, in_specs=(spec,) * 4 + (P(),), out_specs=spec, check_vma=False
    )
```

```python
import jax
import jax.numpy as jnp
from jax import lax
from jax.experimental import pallas as pl
from jax.experimental.pallas import tpu as pltpu
from jax.sharding import Mesh, PartitionSpec as P

NX, NY, NC, NZ = 4, 8, 2, 8
NH, ROWS, DEPTH = 3, 48, 384
HALF = NY // 2 * ROWS
BLOCK = (2, NH, ROWS, DEPTH)
PIECE = (NH, ROWS, DEPTH)
VMEM = pl.BlockSpec(memory_space=pltpu.VMEM)
SMEM = pl.BlockSpec(memory_space=pltpu.SMEM)
ANY = pl.BlockSpec(memory_space=pl.ANY)
PARAMS = pltpu.CompilerParams(vmem_limit_bytes=32 * 2**20)
BF16 = jnp.bfloat16


def left_kernel(place, amp, cross, _, out):
    k = place[NH + 3] * DEPTH + lax.broadcasted_iota(jnp.int32, (1, DEPTH), 1)
    for h in range(NH):
        live = k < place[h]
        for pair, ref in enumerate((amp, cross)):
            block = jnp.where(live, ref[h], jnp.zeros_like(ref[h]))
            for e in range(NX):
                out[e, pair, h] = block


def copy_kernel(src, _, out):
    out[...] = src[...]


def tile_kernel(place, own, other, *refs):
    rights, (out, lhs, rhs) = refs[:NY], refs[NY:]
    y, c = place[NH + 1], place[NH + 2]
    for x in range(NX):
        for h in range(NH):
            for pair in range(2):
                lhs[h, pair, 2 * x + c] = own[x, pair, h]
                lhs[h, pair, 2 * x + 1 - c] = other[x, pair, h]
    for d in range(NY):
        yy = lax.rem(y + d, NY)
        for h in range(NH):
            for pair in range(2):
                rhs[h, pair, yy] = rights[d][pair, h]
    for h in range(NH):
        total = None
        for pair in range(2):
            part = lax.dot_general(
                lhs[h, pair].reshape(NX * NC * ROWS, DEPTH),
                rhs[h, pair].reshape(NY * ROWS, DEPTH),
                (((1,), (1,)), ((), ())),
                preferred_element_type=jnp.float32,
            )
            total = part if total is None else total + part
        total = total.astype(BF16)
        for p in range(NZ):
            out[p, h] = total[p * ROWS : (p + 1) * ROWS]


def sum_kernel(place, pieces, out0, out1):
    x, y, c, z = (place[NH + i] for i in range(4))
    lane = lax.broadcasted_iota(jnp.int32, (1, DEPTH), 1)
    yy = lax.div(lane, ROWS)
    b = ((x * NY + yy) * NC + c) * ROWS + lax.rem(lane, ROWS)
    row = lax.broadcasted_iota(jnp.int32, (ROWS, 1), 0)
    a = ((lax.div(z, NC) * NY + y) * NC + lax.rem(z, NC)) * ROWS + row
    src = lax.broadcasted_iota(jnp.int32, (DEPTH, DEPTH), 0)
    dst = lax.broadcasted_iota(jnp.int32, (DEPTH, DEPTH), 1)
    want = lax.div(dst, NC * ROWS) * ROWS + lax.rem(dst, ROWS)
    mine = lax.rem(lax.div(dst, ROWS), NC) == c
    for k, out in enumerate((out0, out1)):
        half = lax.rem(c + k, 2)
        order = (mine & (src == want + half * HALF)).astype(BF16)
        for h in range(NH):
            total = pieces[0, h].astype(jnp.float32)
            for r in range(1, NZ):
                total = total + pieces[r, h].astype(jnp.float32)
            live = (a < place[h]) & (b < place[h])
            total = jnp.where(live, total, 0.0).astype(BF16)
            out[h] = jnp.dot(total, order, preferred_element_type=jnp.float32).astype(BF16)


def kernel(body, shapes, specs, scratch=(), flops=0):
    many = isinstance(shapes, list)
    make = lambda s: jax.ShapeDtypeStruct(s, BF16)
    return pl.pallas_call(
        body,
        out_shape=[make(s) for s in shapes] if many else make(shapes),
        in_specs=specs,
        out_specs=[VMEM] * len(shapes) if many else VMEM,
        scratch_shapes=[pltpu.VMEM(s, BF16) for s in scratch],
        compiler_params=PARAMS,
        cost_estimate=pl.CostEstimate(flops=flops, bytes_accessed=2**21, transcendentals=0),
    )


def shift(n, d):
    return [((i + d) % n, i) for i in range(n)]


def local(amplitudes, crossed, coulomb, exchange_int, block_order):
    place = [lax.axis_index(n) for n in ("x", "y", "c", "z")]
    place = jnp.concatenate([block_order, jnp.stack(place).astype(jnp.int32)])

    r = {0: jnp.stack([coulomb, exchange_int])}
    for d in (1, 2, 3):
        r[d] = lax.ppermute(r[d - 1], "y", shift(NY, 1))
        r[-d] = lax.ppermute(r[1 - d], "y", shift(NY, -1))
    r[4] = jnp.stack(
        [
            lax.ppermute(r[3][0], "y", shift(NY, 1)),
            lax.ppermute(r[-3][1], "y", shift(NY, -1)),
        ]
    )
    left = kernel(left_kernel, (NX,) + BLOCK, [SMEM, VMEM, VMEM, ANY])(
        place, amplitudes, crossed, r[0]
    )
    own = lax.all_to_all(left, "x", 0, 0, tiled=True)
    other = kernel(copy_kernel, (NX,) + BLOCK, [VMEM, ANY])(own, r[2])
    other = lax.ppermute(other, "c", shift(NC, 1))
    rights = [r[0], r[1], r[2], r[3], r[4], r[-3], r[-2], r[-1]]

    pieces = kernel(
        tile_kernel,
        (NZ,) + PIECE,
        [SMEM] + [VMEM] * (2 + NY),
        [(NH, 2, NX * NC, ROWS, DEPTH), (NH, 2, NY, ROWS, DEPTH)],
        flops=8 * NH * (NY * ROWS) ** 2 * DEPTH,
    )(place, own, other, *rights)
    pieces = lax.all_to_all(pieces, "z", 0, 0, tiled=True)
    halves = kernel(sum_kernel, [PIECE, PIECE], [SMEM, VMEM])(place, pieces)
    result = None
    for k, part in enumerate(halves):
        moves = []
        for x in range(NX):
            for c in range(NC):
                for z in range(NZ):
                    to = z * NZ + x * 2 + (c + k) % 2
                    moves.append(((x * NC + c) * NZ + z, to))
        part = lax.ppermute(part, ("x", "c", "z"), moves)
        result = part if result is None else result + part
    return result


def solution(mesh):
    grid = Mesh(mesh.devices.reshape(NX, NY, NC, NZ), ("x", "y", "c", "z"))
    spec = P(None, ("x", "y", "c"), "z")
    return jax.shard_map(
        local, mesh=grid, in_specs=(spec,) * 4 + (P(),), out_specs=spec, check_vma=False
    )
```

```python
import jax
import jax.numpy as jnp
from jax import lax
from jax.experimental import pallas as pl
from jax.experimental.pallas import tpu as pltpu
from jax.sharding import Mesh, PartitionSpec as P

NX, NF, NQ, NC, NZ = 4, 2, 4, 2, 8
AXES = ("x", "f", "q", "c", "z")
NH, ROWS, DEPTH = 3, 48, 384
BLOCK = (2, NH, ROWS, DEPTH)
PIECE = (NH, ROWS, DEPTH)
NP = NQ * NC
LANES = 128
LAST = 2 * ROWS
KEPT = LANES - LAST
LEFT = ROWS - KEPT
GROUP = 8
PACKED = (ROWS + GROUP, LANES)
VMEM = pl.BlockSpec(memory_space=pltpu.VMEM)
SMEM = pl.BlockSpec(memory_space=pltpu.SMEM)
PARAMS = pltpu.CompilerParams(vmem_limit_bytes=32 * 2**20)
BF16 = jnp.bfloat16


def left_kernel(place, amp, cross, out):
    k = place[NH + 4] * DEPTH + lax.broadcasted_iota(jnp.int32, (1, DEPTH), 1)
    for h in range(NH):
        live = k < place[h]
        for pair, ref in enumerate((amp, cross)):
            block = jnp.where(live, ref[h], jnp.zeros_like(ref[h]))
            out[pair, h] = block


def tile_kernel(place, own, other, near, far, out, lhs, rhs):
    f, c = place[NH + 1], place[NH + 3]
    for q in range(NQ):
        for h in range(NH):
            for pair in range(2):
                lhs[h, pair, 2 * q + c] = own[q, pair, h]
                lhs[h, pair, 2 * q + 1 - c] = other[q, pair, h]
    for x in range(NX):
        for h in range(NH):
            for pair in range(2):
                rhs[h, pair, 2 * x + f] = near[x, pair, h]
                rhs[h, pair, 2 * x + 1 - f] = far[x, pair, h]
    totals = []
    for h in range(NH):
        total = None
        for pair in range(2):
            part = lax.dot_general(
                lhs[h, pair].reshape(NP * ROWS, DEPTH),
                rhs[h, pair].reshape(NZ * ROWS, DEPTH),
                (((1,), (1,)), ((), ())),
                preferred_element_type=jnp.float32,
            )
            total = part if total is None else total + part
        totals.append(total)
    fill = jnp.zeros((GROUP, LANES - ROWS // GROUP * LEFT), jnp.float32)
    for p in range(NP):
        rows = [t[p * ROWS : (p + 1) * ROWS] for t in totals]
        for z in range(NZ):
            at = z * ROWS
            main = jnp.concatenate(
                [rows[0][:, at : at + ROWS], rows[1][:, at : at + ROWS], rows[2][:, at : at + KEPT]], axis=1
            )
            rest = rows[2][:, at + KEPT : at + ROWS]
            rest = [rest[g : g + GROUP] for g in range(0, ROWS, GROUP)]
            rest = jnp.concatenate(rest + [fill], axis=1)
            out[p * NZ + z] = jnp.concatenate([main, rest], axis=0).astype(BF16)


def sum_kernel(place, pieces, out):
    x, f, q, c, z = (place[NH + i] for i in range(5))
    straight = lax.rem(z, 2) == f
    sums = []
    for s in range(NP):
        total = pieces[s * NZ].astype(jnp.float32)
        for r in range(1, NZ):
            total = total + pieces[s * NZ + r].astype(jnp.float32)
        sums.append(total)
    b = z * DEPTH + lax.broadcasted_iota(jnp.int32, (1, DEPTH), 1)
    a = (((x * NF + f) * NQ + q) * NC + c) * ROWS + lax.broadcasted_iota(jnp.int32, (ROWS, 1), 0)
    blocks = [[] for _ in range(NH)]
    for s in range(NP):
        mirrored = (NQ - 1 - s // NC) * NC + s % NC
        total = jnp.where(straight, sums[s], sums[mirrored])
        rest = [total[ROWS:, g * LEFT : (g + 1) * LEFT] for g in range(ROWS // GROUP)]
        rest = jnp.concatenate(rest, axis=0)
        blocks[0].append(total[:ROWS, :ROWS])
        blocks[1].append(total[:ROWS, ROWS:LAST])
        blocks[2].append(jnp.concatenate([total[:ROWS, LAST:], rest], axis=1))
    for h in range(NH):
        live = (a < place[h]) & (b < place[h])
        whole = jnp.concatenate(blocks[h], axis=1)
        out[h] = jnp.where(live, whole, 0.0).astype(BF16)


def kernel(body, shape, specs, scratch=(), flops=0):
    return pl.pallas_call(
        body,
        out_shape=jax.ShapeDtypeStruct(shape, BF16),
        in_specs=specs,
        out_specs=VMEM,
        scratch_shapes=[pltpu.VMEM(s, BF16) for s in scratch],
        compiler_params=PARAMS,
        cost_estimate=pl.CostEstimate(flops=flops, bytes_accessed=2**21, transcendentals=0),
    )


def local(amplitudes, crossed, coulomb, exchange_int, block_order):
    place = [lax.axis_index(n) for n in AXES]
    place = jnp.concatenate([block_order, jnp.stack(place).astype(jnp.int32)])

    def along_x(block):
        return lax.all_to_all(jnp.broadcast_to(block, (NX,) + BLOCK), "x", 0, 0, tiled=True)

    right = jnp.stack([coulomb, exchange_int])
    n = NF * NQ
    mirror = lax.ppermute(right, ("f", "q"), [(i, n - 1 - i) for i in range(n)])
    near = along_x(right)
    left = kernel(left_kernel, BLOCK, [SMEM, VMEM, VMEM])(place, amplitudes, crossed)
    own = lax.all_gather(left, "q")
    far = along_x(mirror)
    other = lax.ppermute(own, "c", [(0, 1), (1, 0)])
    pieces = kernel(
        tile_kernel,
        (NP * NZ,) + PACKED,
        [SMEM] + [VMEM] * 4,
        [(NH, 2, NP, ROWS, DEPTH), (NH, 2, NZ, ROWS, DEPTH)],
        flops=8 * NH * (NP * ROWS) ** 2 * DEPTH,
    )(place, own, other, near, far)
    pieces = lax.all_to_all(pieces, ("q", "c", "z"), 0, 0, tiled=True)
    return kernel(sum_kernel, PIECE, [SMEM, VMEM])(place, pieces)


def solution(mesh):
    grid = Mesh(mesh.devices.reshape(NX, NF, NQ, NC, NZ), AXES)
    spec = P(None, AXES[:4], "z")
    return jax.shard_map(
        local, mesh=grid, in_specs=(spec,) * 4 + (P(),), out_specs=spec, check_vma=False
    )
```

```python
import jax
import jax.numpy as jnp
from jax import lax
from jax.experimental import pallas as pl
from jax.experimental.pallas import tpu as pltpu
from jax.sharding import Mesh, PartitionSpec as P

NX, NF, NQ, NC, NZ = 4, 2, 4, 2, 8
AXES = ("x", "f", "q", "c", "z")
NH, ROWS, DEPTH = 3, 48, 384
BLOCK = (2, NH, ROWS, DEPTH)
PIECE = (NH, ROWS, DEPTH)
NP = NQ * NC
LANES = 128
LAST = 2 * ROWS
KEPT = LANES - LAST
LEFT = ROWS - KEPT
GROUP = 8
PACKED = (ROWS + GROUP, LANES)
VMEM = pl.BlockSpec(memory_space=pltpu.VMEM)
ANY = pl.BlockSpec(memory_space=pl.ANY)
SMEM = pl.BlockSpec(memory_space=pltpu.SMEM)
PARAMS = pltpu.CompilerParams(vmem_limit_bytes=32 * 2**20)
BF16 = jnp.bfloat16


def spread_kernel(mirror, amp, cross, _, spread, left):
    for e in range(NX):
        spread[e] = mirror[...]
    left[0] = amp[...]
    left[1] = cross[...]


def mask_kernel(place, rows, _, out):
    k = place[NH + 4] * DEPTH + lax.broadcasted_iota(jnp.int32, (1, DEPTH), 1)
    for h in range(NH):
        live = k < place[h]
        for q in range(NQ):
            for pair in range(2):
                block = rows[q, pair, h]
                out[q, pair, h] = jnp.where(live, block, jnp.zeros_like(block))


def tile_kernel(place, rows, near, far, *rest):
    before, (out, lhs, rhs) = rest[:-3], rest[-3:]
    f, c = place[NH + 1], place[NH + 3]
    if before:
        for q in range(NQ):
            for z in range(NZ):
                out[(q * NC + c) * NZ + z] = before[0][q * NZ + z]
    for q in range(NQ):
        for h in range(NH):
            for pair in range(2):
                lhs[h, pair, q] = rows[q, pair, h]
    for x in range(NX):
        for h in range(NH):
            for pair in range(2):
                rhs[h, pair, 2 * x + f] = near[x, pair, h]
                rhs[h, pair, 2 * x + 1 - f] = far[x, pair, h]
    totals = []
    for h in range(NH):
        total = None
        for pair in range(2):
            part = lax.dot_general(
                lhs[h, pair].reshape(NQ * ROWS, DEPTH),
                rhs[h, pair].reshape(NZ * ROWS, DEPTH),
                (((1,), (1,)), ((), ())),
                preferred_element_type=jnp.float32,
            )
            total = part if total is None else total + part
        totals.append(total)
    fill = jnp.zeros((GROUP, LANES - ROWS // GROUP * LEFT), jnp.float32)
    for p in range(NQ):
        rows = [t[p * ROWS : (p + 1) * ROWS] for t in totals]
        for z in range(NZ):
            at = z * ROWS
            main = jnp.concatenate(
                [rows[0][:, at : at + ROWS], rows[1][:, at : at + ROWS], rows[2][:, at : at + KEPT]], axis=1
            )
            rest = rows[2][:, at + KEPT : at + ROWS]
            rest = [rest[g : g + GROUP] for g in range(0, ROWS, GROUP)]
            rest = jnp.concatenate(rest + [fill], axis=1)
            out[((p * NC + 1 - c) if before else p) * NZ + z] = jnp.concatenate([main, rest], axis=0).astype(BF16)


def sum_kernel(place, pieces, out):
    x, f, q, c, z = (place[NH + i] for i in range(5))
    straight = lax.rem(z, 2) == f
    sums = []
    for s in range(NP):
        total = pieces[s * NZ].astype(jnp.float32)
        for r in range(1, NZ):
            total = total + pieces[s * NZ + r].astype(jnp.float32)
        sums.append(total)
    b = z * DEPTH + lax.broadcasted_iota(jnp.int32, (1, DEPTH), 1)
    a = (((x * NF + f) * NQ + q) * NC + c) * ROWS + lax.broadcasted_iota(jnp.int32, (ROWS, 1), 0)
    blocks = [[] for _ in range(NH)]
    for s in range(NP):
        mirrored = (NQ - 1 - s // NC) * NC + s % NC
        total = jnp.where(straight, sums[s], sums[mirrored])
        rest = [total[ROWS:, g * LEFT : (g + 1) * LEFT] for g in range(ROWS // GROUP)]
        rest = jnp.concatenate(rest, axis=0)
        blocks[0].append(total[:ROWS, :ROWS])
        blocks[1].append(total[:ROWS, ROWS:LAST])
        blocks[2].append(jnp.concatenate([total[:ROWS, LAST:], rest], axis=1))
    for h in range(NH):
        live = (a < place[h]) & (b < place[h])
        whole = jnp.concatenate(blocks[h], axis=1)
        out[h] = jnp.where(live, whole, 0.0).astype(BF16)


def kernel(body, shapes, specs, scratch=(), flops=0):
    make = lambda shape: jax.ShapeDtypeStruct(shape, BF16)
    many = isinstance(shapes, list)
    return pl.pallas_call(
        body,
        out_shape=[make(shape) for shape in shapes] if many else make(shapes),
        in_specs=specs,
        out_specs=[VMEM] * len(shapes) if many else VMEM,
        scratch_shapes=[pltpu.VMEM(shape, BF16) for shape in scratch],
        compiler_params=PARAMS,
        cost_estimate=pl.CostEstimate(flops=flops, bytes_accessed=2**21, transcendentals=0),
    )


def local(amplitudes, crossed, coulomb, exchange_int, block_order):
    place = [lax.axis_index(n) for n in AXES]
    place = jnp.concatenate([block_order, jnp.stack(place).astype(jnp.int32)])

    right = jnp.stack([coulomb, exchange_int])
    n = NF * NQ
    mirror = lax.ppermute(right, ("f", "q"), [(i, n - 1 - i) for i in range(n)])
    near = lax.all_gather(right, "x")
    spread, left = kernel(spread_kernel, [(NX,) + BLOCK, BLOCK], [VMEM] * 3 + [ANY])(
        mirror, amplitudes, crossed, near
    )
    far = lax.all_to_all(spread, "x", 0, 0, tiled=True)
    own = lax.all_gather(left, "q")
    own = kernel(mask_kernel, (NQ,) + BLOCK, [SMEM, VMEM, ANY])(place, own, far)
    other = lax.ppermute(own, "c", [(0, 1), (1, 0)])
    pieces = []
    for rows, count in ((own, NQ * NZ), (other, NP * NZ)):
        pieces = kernel(
            tile_kernel,
            (count,) + PACKED,
            [SMEM] + [VMEM] * (3 + len(pieces)),
            [(NH, 2, NQ, ROWS, DEPTH), (NH, 2, NZ, ROWS, DEPTH)],
            flops=4 * NH * (NP * ROWS) ** 2 * DEPTH,
        )(place, rows, near, far, *pieces)
        pieces = [pieces]
    pieces = pieces[0]
    pieces = lax.all_to_all(pieces, ("q", "c", "z"), 0, 0, tiled=True)
    return kernel(sum_kernel, PIECE, [SMEM, VMEM])(place, pieces)


def solution(mesh):
    grid = Mesh(mesh.devices.reshape(NX, NF, NQ, NC, NZ), AXES)
    spec = P(None, AXES[:4], "z")
    return jax.shard_map(
        local, mesh=grid, in_specs=(spec,) * 4 + (P(),), out_specs=spec, check_vma=False
    )
```

```python
import jax
import jax.numpy as jnp
from jax import lax
from jax.experimental import pallas as pl
from jax.experimental.pallas import tpu as pltpu
from jax.sharding import Mesh, PartitionSpec as P

NX, NF, NQ, NC, NZ = 4, 2, 4, 2, 8
AXES = ("x", "f", "q", "c", "z")
NH, ROWS, DEPTH = 3, 48, 384
BLOCK = (2, NH, ROWS, DEPTH)
PIECE = (NH, ROWS, DEPTH)
NP = NQ * NC
LANES = 128
LAST = 2 * ROWS
KEPT = LANES - LAST
LEFT = ROWS - KEPT
GROUP = 8
PACKED = (ROWS + GROUP, LANES)
VMEM = pl.BlockSpec(memory_space=pltpu.VMEM)
ANY = pl.BlockSpec(memory_space=pl.ANY)
SMEM = pl.BlockSpec(memory_space=pltpu.SMEM)
PARAMS = pltpu.CompilerParams(vmem_limit_bytes=32 * 2**20)
BF16 = jnp.bfloat16


def left_kernel(amp, cross, out):
    for q in range(NQ):
        out[q, 0] = amp[...]
        out[q, 1] = cross[...]


def copy_kernel(src, _, out):
    out[...] = src[...]


def mask_kernel(place, rows, _, out):
    k = place[NH + 4] * DEPTH + lax.broadcasted_iota(jnp.int32, (1, DEPTH), 1)
    for h in range(NH):
        live = k < place[h]
        for q in range(NQ):
            for pair in range(2):
                block = rows[q, pair, h]
                out[q, pair, h] = jnp.where(live, block, jnp.zeros_like(block))


def tile_kernel(place, rows, near, far, *rest):
    before, (out, lhs, rhs) = rest[:-3], rest[-3:]
    f, c = place[NH + 1], place[NH + 3]
    if before:
        for q in range(NQ):
            for z in range(NZ):
                out[(q * NC + c) * NZ + z] = before[0][q * NZ + z]
    for q in range(NQ):
        for h in range(NH):
            for pair in range(2):
                lhs[h, pair, q] = rows[q, pair, h]
    for x in range(NX):
        for h in range(NH):
            for pair in range(2):
                rhs[h, pair, 2 * x + f] = near[x, pair, h]
                rhs[h, pair, 2 * x + 1 - f] = far[x, pair, h]
    totals = []
    for h in range(NH):
        total = None
        for pair in range(2):
            part = lax.dot_general(
                lhs[h, pair].reshape(NQ * ROWS, DEPTH),
                rhs[h, pair].reshape(NZ * ROWS, DEPTH),
                (((1,), (1,)), ((), ())),
                preferred_element_type=jnp.float32,
            )
            total = part if total is None else total + part
        totals.append(total)
    fill = jnp.zeros((GROUP, LANES - ROWS // GROUP * LEFT), jnp.float32)
    for p in range(NQ):
        rows = [t[p * ROWS : (p + 1) * ROWS] for t in totals]
        for z in range(NZ):
            at = z * ROWS
            main = jnp.concatenate(
                [rows[0][:, at : at + ROWS], rows[1][:, at : at + ROWS], rows[2][:, at : at + KEPT]], axis=1
            )
            rest = rows[2][:, at + KEPT : at + ROWS]
            rest = [rest[g : g + GROUP] for g in range(0, ROWS, GROUP)]
            rest = jnp.concatenate(rest + [fill], axis=1)
            out[((p * NC + 1 - c) if before else p) * NZ + z] = jnp.concatenate([main, rest], axis=0).astype(BF16)


def sum_kernel(place, pieces, out):
    x, f, q, c, z = (place[NH + i] for i in range(5))
    straight = lax.rem(z, 2) == f
    sums = []
    for s in range(NP):
        total = pieces[s * NZ].astype(jnp.float32)
        for r in range(1, NZ):
            total = total + pieces[s * NZ + r].astype(jnp.float32)
        sums.append(total)
    b = z * DEPTH + lax.broadcasted_iota(jnp.int32, (1, DEPTH), 1)
    a = (((x * NF + f) * NQ + q) * NC + c) * ROWS + lax.broadcasted_iota(jnp.int32, (ROWS, 1), 0)
    blocks = [[] for _ in range(NH)]
    for s in range(NP):
        mirrored = (NQ - 1 - s // NC) * NC + s % NC
        total = jnp.where(straight, sums[s], sums[mirrored])
        rest = [total[ROWS:, g * LEFT : (g + 1) * LEFT] for g in range(ROWS // GROUP)]
        rest = jnp.concatenate(rest, axis=0)
        blocks[0].append(total[:ROWS, :ROWS])
        blocks[1].append(total[:ROWS, ROWS:LAST])
        blocks[2].append(jnp.concatenate([total[:ROWS, LAST:], rest], axis=1))
    for h in range(NH):
        live = (a < place[h]) & (b < place[h])
        whole = jnp.concatenate(blocks[h], axis=1)
        out[h] = jnp.where(live, whole, 0.0).astype(BF16)


def kernel(body, shapes, specs, scratch=(), flops=0):
    make = lambda shape: jax.ShapeDtypeStruct(shape, BF16)
    many = isinstance(shapes, list)
    return pl.pallas_call(
        body,
        out_shape=[make(shape) for shape in shapes] if many else make(shapes),
        in_specs=specs,
        out_specs=[VMEM] * len(shapes) if many else VMEM,
        scratch_shapes=[pltpu.VMEM(shape, BF16) for shape in scratch],
        compiler_params=PARAMS,
        cost_estimate=pl.CostEstimate(flops=flops, bytes_accessed=2**21, transcendentals=0),
    )


def local(amplitudes, crossed, coulomb, exchange_int, block_order):
    place = [lax.axis_index(n) for n in AXES]
    place = jnp.concatenate([block_order, jnp.stack(place).astype(jnp.int32)])

    right = jnp.stack([coulomb, exchange_int])
    n = NF * NQ
    mirror = lax.ppermute(right, ("f", "q"), [(i, n - 1 - i) for i in range(n)])
    near = lax.all_gather(right, "x")
    left = kernel(left_kernel, (NQ,) + BLOCK, [VMEM] * 2)(amplitudes, crossed)
    own = lax.all_to_all(left, "q", 0, 0, tiled=True)
    mirror = kernel(copy_kernel, BLOCK, [VMEM, ANY], flops=3 * 10**10)(mirror, near)
    far = lax.all_gather(mirror, "x")
    own = kernel(mask_kernel, (NQ,) + BLOCK, [SMEM, VMEM, ANY])(place, own, far)
    other = lax.ppermute(own, "c", [(0, 1), (1, 0)])
    pieces = []
    for rows, count in ((own, NQ * NZ), (other, NP * NZ)):
        pieces = kernel(
            tile_kernel,
            (count,) + PACKED,
            [SMEM] + [VMEM] * (3 + len(pieces)),
            [(NH, 2, NQ, ROWS, DEPTH), (NH, 2, NZ, ROWS, DEPTH)],
            flops=4 * NH * (NP * ROWS) ** 2 * DEPTH,
        )(place, rows, near, far, *pieces)
        pieces = [pieces]
    pieces = pieces[0]
    pieces = lax.all_to_all(pieces, ("q", "c", "z"), 0, 0, tiled=True)
    return kernel(sum_kernel, PIECE, [SMEM, VMEM])(place, pieces)


def solution(mesh):
    grid = Mesh(mesh.devices.reshape(NX, NF, NQ, NC, NZ), AXES)
    spec = P(None, AXES[:4], "z")
    return jax.shard_map(
        local, mesh=grid, in_specs=(spec,) * 4 + (P(),), out_specs=spec, check_vma=False
    )
```

```python
import jax
import jax.numpy as jnp
from jax import lax
from jax.experimental import pallas as pl
from jax.experimental.pallas import tpu as pltpu
from jax.sharding import Mesh, PartitionSpec as P

NX, NF, NQ, NC, NZ = 4, 2, 4, 2, 8
AXES = ("x", "f", "q", "c", "z")
NH, ROWS, DEPTH = 3, 48, 384
BLOCK = (2, NH, ROWS, DEPTH)
PIECE = (NH, ROWS, DEPTH)
NP = NQ * NC
LANES = 128
LAST = 2 * ROWS
KEPT = LANES - LAST
LEFT = ROWS - KEPT
GROUP = 8
PACKED = (ROWS + GROUP, LANES)
VMEM = pl.BlockSpec(memory_space=pltpu.VMEM)
ANY = pl.BlockSpec(memory_space=pl.ANY)
SMEM = pl.BlockSpec(memory_space=pltpu.SMEM)
PARAMS = pltpu.CompilerParams(vmem_limit_bytes=32 * 2**20)
BF16 = jnp.bfloat16


def left_kernel(amp, cross, out):
    for q in range(NQ):
        out[q, 0] = amp[...]
        out[q, 1] = cross[...]


def copy_kernel(src, _, out):
    out[...] = src[...]


def mask_kernel(place, rows, *rest):
    out = rest[-1]
    k = place[NH + 4] * DEPTH + lax.broadcasted_iota(jnp.int32, (1, DEPTH), 1)
    for h in range(NH):
        live = k < place[h]
        for q in range(NQ):
            for pair in range(2):
                block = rows[q, pair, h]
                out[q, pair, h] = jnp.where(live, block, jnp.zeros_like(block))


def tile_kernel(place, rows, far, *rest):
    near, before, (out, lhs, rhs) = rest[:NX], rest[NX:-3], rest[-3:]
    x0, f, c = place[NH], place[NH + 1], place[NH + 3]
    if before:
        for q in range(NQ):
            for z in range(NZ):
                out[(q * NC + c) * NZ + z] = before[0][q * NZ + z]
    for q in range(NQ):
        for h in range(NH):
            for pair in range(2):
                lhs[h, pair, q] = rows[q, pair, h]
    for x in range(NX):
        for h in range(NH):
            for pair in range(2):
                rhs[h, pair, 2 * lax.rem(x0 + x, NX) + f] = near[x][pair, h]
                rhs[h, pair, 2 * x + 1 - f] = far[x, pair, h]
    totals = []
    for h in range(NH):
        total = None
        for pair in range(2):
            part = lax.dot_general(
                lhs[h, pair].reshape(NQ * ROWS, DEPTH),
                rhs[h, pair].reshape(NZ * ROWS, DEPTH),
                (((1,), (1,)), ((), ())),
                preferred_element_type=jnp.float32,
            )
            total = part if total is None else total + part
        totals.append(total)
    fill = jnp.zeros((GROUP, LANES - ROWS // GROUP * LEFT), jnp.float32)
    for p in range(NQ):
        rows = [t[p * ROWS : (p + 1) * ROWS] for t in totals]
        for z in range(NZ):
            at = z * ROWS
            main = jnp.concatenate(
                [rows[0][:, at : at + ROWS], rows[1][:, at : at + ROWS], rows[2][:, at : at + KEPT]], axis=1
            )
            rest = rows[2][:, at + KEPT : at + ROWS]
            rest = [rest[g : g + GROUP] for g in range(0, ROWS, GROUP)]
            rest = jnp.concatenate(rest + [fill], axis=1)
            out[((p * NC + 1 - c) if before else p) * NZ + z] = jnp.concatenate([main, rest], axis=0).astype(BF16)


def sum_kernel(place, pieces, out):
    x, f, q, c, z = (place[NH + i] for i in range(5))
    straight = lax.rem(z, 2) == f
    sums = []
    for s in range(NP):
        total = pieces[s * NZ].astype(jnp.float32)
        for r in range(1, NZ):
            total = total + pieces[s * NZ + r].astype(jnp.float32)
        sums.append(total)
    b = z * DEPTH + lax.broadcasted_iota(jnp.int32, (1, DEPTH), 1)
    a = (((x * NF + f) * NQ + q) * NC + c) * ROWS + lax.broadcasted_iota(jnp.int32, (ROWS, 1), 0)
    blocks = [[] for _ in range(NH)]
    for s in range(NP):
        mirrored = (NQ - 1 - s // NC) * NC + s % NC
        total = jnp.where(straight, sums[s], sums[mirrored])
        rest = [total[ROWS:, g * LEFT : (g + 1) * LEFT] for g in range(ROWS // GROUP)]
        rest = jnp.concatenate(rest, axis=0)
        blocks[0].append(total[:ROWS, :ROWS])
        blocks[1].append(total[:ROWS, ROWS:LAST])
        blocks[2].append(jnp.concatenate([total[:ROWS, LAST:], rest], axis=1))
    for h in range(NH):
        live = (a < place[h]) & (b < place[h])
        whole = jnp.concatenate(blocks[h], axis=1)
        out[h] = jnp.where(live, whole, 0.0).astype(BF16)


def kernel(body, shapes, specs, scratch=(), flops=0):
    make = lambda shape: jax.ShapeDtypeStruct(shape, BF16)
    many = isinstance(shapes, list)
    return pl.pallas_call(
        body,
        out_shape=[make(shape) for shape in shapes] if many else make(shapes),
        in_specs=specs,
        out_specs=[VMEM] * len(shapes) if many else VMEM,
        scratch_shapes=[pltpu.VMEM(shape, BF16) for shape in scratch],
        compiler_params=PARAMS,
        cost_estimate=pl.CostEstimate(flops=flops, bytes_accessed=2**21, transcendentals=0),
    )


def local(amplitudes, crossed, coulomb, exchange_int, block_order):
    place = [lax.axis_index(n) for n in AXES]
    place = jnp.concatenate([block_order, jnp.stack(place).astype(jnp.int32)])

    right = jnp.stack([coulomb, exchange_int])
    n = NF * NQ
    mirror = lax.ppermute(right, ("f", "q"), [(i, n - 1 - i) for i in range(n)])
    near = [right] + [
        lax.ppermute(right, "x", [((i + e) % NX, i) for i in range(NX)]) for e in range(1, NX)
    ]
    left = kernel(left_kernel, (NQ,) + BLOCK, [VMEM] * 2)(amplitudes, crossed)
    own = lax.all_to_all(left, "q", 0, 0, tiled=True)
    mirror = kernel(copy_kernel, BLOCK, [VMEM, ANY], flops=10**10)(mirror, right)
    far = lax.all_gather(mirror, "x")
    own = kernel(mask_kernel, (NQ,) + BLOCK, [SMEM, VMEM] + [ANY] * (1 + NX))(
        place, own, far, *near
    )
    other = lax.ppermute(own, "c", [(0, 1), (1, 0)])
    pieces = []
    for rows, count in ((own, NQ * NZ), (other, NP * NZ)):
        pieces = kernel(
            tile_kernel,
            (count,) + PACKED,
            [SMEM] + [VMEM] * (2 + NX + len(pieces)),
            [(NH, 2, NQ, ROWS, DEPTH), (NH, 2, NZ, ROWS, DEPTH)],
            flops=4 * NH * (NP * ROWS) ** 2 * DEPTH,
        )(place, rows, far, *near, *pieces)
        pieces = [pieces]
    pieces = pieces[0]
    pieces = lax.all_to_all(pieces, ("q", "c", "z"), 0, 0, tiled=True)
    return kernel(sum_kernel, PIECE, [SMEM, VMEM])(place, pieces)


def solution(mesh):
    grid = Mesh(mesh.devices.reshape(NX, NF, NQ, NC, NZ), AXES)
    spec = P(None, AXES[:4], "z")
    return jax.shard_map(
        local, mesh=grid, in_specs=(spec,) * 4 + (P(),), out_specs=spec, check_vma=False
    )
```

```python
import jax
import jax.numpy as jnp
from jax import lax
from jax.experimental import pallas as pl
from jax.experimental.pallas import tpu as pltpu
from jax.sharding import Mesh, PartitionSpec as P

NX, NF, NQ, NC, NZ = 4, 2, 4, 2, 8
AXES = ("x", "f", "q", "c", "z")
NH, ROWS, DEPTH = 3, 48, 384
BLOCK = (2, NH, ROWS, DEPTH)
PIECE = (NH, ROWS, DEPTH)
NP = NQ * NC
LANES = 128
LAST = 2 * ROWS
KEPT = LANES - LAST
LEFT = ROWS - KEPT
GROUP = 8
PACKED = (ROWS + GROUP, LANES)
VMEM = pl.BlockSpec(memory_space=pltpu.VMEM)
ANY = pl.BlockSpec(memory_space=pl.ANY)
SMEM = pl.BlockSpec(memory_space=pltpu.SMEM)
PARAMS = pltpu.CompilerParams(vmem_limit_bytes=32 * 2**20)
BF16 = jnp.bfloat16


def left_kernel(amp, cross, out):
    for q in range(NQ):
        out[q, 0] = amp[...]
        out[q, 1] = cross[...]


def copy_kernel(src, _, out):
    out[...] = src[...]


def mask_kernel(order, place, rows, *rest):
    out = rest[-1]
    k = place[4] * DEPTH + lax.broadcasted_iota(jnp.int32, (1, DEPTH), 1)
    for h in range(NH):
        live = k < order[h]
        for q in range(NQ):
            for pair in range(2):
                block = rows[q, pair, h]
                out[pair, h, q] = jnp.where(live, block, jnp.zeros_like(block))


def columns(place, near, far, rhs):
    x0, f = place[0], place[1]
    for x in range(NX):
        for h in range(NH):
            for pair in range(2):
                rhs[h, pair, 2 * lax.rem(x0 + x, NX) + f] = near[x][pair, h]
                rhs[h, pair, 2 * lax.rem(x0 + x, NX) + 1 - f] = far[x][pair, h]


def first_kernel(place, rows, *rest):
    near, far, (out, rhs) = rest[:NX], rest[NX : 2 * NX], rest[2 * NX :]
    columns(place, near, far, rhs)
    tile(rows, rhs, out, lambda q: q)


def second_kernel(place, rows, *rest):
    near, far = rest[:NX], rest[NX : 2 * NX]
    first, out, rhs = rest[2 * NX :]
    columns(place, near, far, rhs)
    c = place[3]
    for q in range(NQ):
        for z in range(NZ):
            out[(q * NC + c) * NZ + z] = first[q * NZ + z]
    tile(rows, rhs, out, lambda q: q * NC + 1 - c)


def tile(rows, rhs, out, at_row):
    totals = []
    for h in range(NH):
        total = None
        for pair in range(2):
            part = lax.dot_general(
                rows[pair, h].reshape(NQ * ROWS, DEPTH),
                rhs[h, pair].reshape(NZ * ROWS, DEPTH),
                (((1,), (1,)), ((), ())),
                preferred_element_type=jnp.float32,
            )
            total = part if total is None else total + part
        totals.append(total)
    fill = jnp.zeros((GROUP, LANES - ROWS // GROUP * LEFT), jnp.float32)
    for q in range(NQ):
        part = [t[q * ROWS : (q + 1) * ROWS] for t in totals]
        for z in range(NZ):
            at = z * ROWS
            main = jnp.concatenate(
                [part[0][:, at : at + ROWS], part[1][:, at : at + ROWS], part[2][:, at : at + KEPT]], axis=1
            )
            rest = part[2][:, at + KEPT : at + ROWS]
            rest = [rest[g : g + GROUP] for g in range(0, ROWS, GROUP)]
            rest = jnp.concatenate(rest + [fill], axis=1)
            out[at_row(q) * NZ + z] = jnp.concatenate([main, rest], axis=0).astype(BF16)


def sum_kernel(order, place, pieces, out):
    x, f, q, c, z = (place[i] for i in range(5))
    straight = lax.rem(z, 2) == f
    sums = []
    for s in range(NP):
        total = pieces[s * NZ].astype(jnp.float32)
        for r in range(1, NZ):
            total = total + pieces[s * NZ + r].astype(jnp.float32)
        sums.append(total)
    b = z * DEPTH + lax.broadcasted_iota(jnp.int32, (1, DEPTH), 1)
    a = (((x * NF + f) * NQ + q) * NC + c) * ROWS + lax.broadcasted_iota(jnp.int32, (ROWS, 1), 0)
    blocks = [[] for _ in range(NH)]
    for s in range(NP):
        mirrored = (NQ - 1 - s // NC) * NC + s % NC
        total = jnp.where(straight, sums[s], sums[mirrored])
        rest = [total[ROWS:, g * LEFT : (g + 1) * LEFT] for g in range(ROWS // GROUP)]
        rest = jnp.concatenate(rest, axis=0)
        blocks[0].append(total[:ROWS, :ROWS])
        blocks[1].append(total[:ROWS, ROWS:LAST])
        blocks[2].append(jnp.concatenate([total[:ROWS, LAST:], rest], axis=1))
    for h in range(NH):
        live = (a < order[h]) & (b < order[h])
        whole = jnp.concatenate(blocks[h], axis=1)
        out[h] = jnp.where(live, whole, 0.0).astype(BF16)


def kernel(body, shapes, specs, scratch=(), flops=0):
    make = lambda shape: jax.ShapeDtypeStruct(shape, BF16)
    many = isinstance(shapes, list)
    return pl.pallas_call(
        body,
        out_shape=[make(shape) for shape in shapes] if many else make(shapes),
        in_specs=specs,
        out_specs=[VMEM] * len(shapes) if many else VMEM,
        scratch_shapes=[pltpu.VMEM(shape, BF16) for shape in scratch],
        compiler_params=PARAMS,
        cost_estimate=pl.CostEstimate(flops=flops, bytes_accessed=2**21, transcendentals=0),
    )


def local(amplitudes, crossed, coulomb, exchange_int, block_order):
    place = [lax.axis_index(n) for n in AXES]
    place = jnp.stack(place).astype(jnp.int32)

    def along_x(block):
        return [block] + [
            lax.ppermute(block, "x", [((i + e) % NX, i) for i in range(NX)]) for e in range(1, NX)
        ]

    right = jnp.stack([coulomb, exchange_int])
    n = NF * NQ
    mirror = lax.ppermute(right, ("f", "q"), [(i, n - 1 - i) for i in range(n)])
    near = along_x(right)
    left = kernel(left_kernel, (NQ,) + BLOCK, [VMEM] * 2)(amplitudes, crossed)
    own = lax.all_to_all(left, "q", 0, 0, tiled=True)
    mirror = kernel(copy_kernel, BLOCK, [VMEM, ANY], flops=10**10)(mirror, right)
    far = along_x(mirror)
    own = kernel(mask_kernel, (2, NH, NQ, ROWS, DEPTH), [SMEM, SMEM, VMEM, ANY])(
        block_order, place, own, right
    )
    other = lax.ppermute(own, "c", [(0, 1), (1, 0)])
    flops = 4 * NH * (NP * ROWS) ** 2 * DEPTH
    scratch = [(NH, 2, NZ, ROWS, DEPTH)]
    specs = [SMEM] + [VMEM] * (1 + 2 * NX)
    first = kernel(first_kernel, (NQ * NZ,) + PACKED, specs, scratch, 12 * 10**9)(
        place, own, *near, *far
    )
    pieces = kernel(second_kernel, (NP * NZ,) + PACKED, specs + [VMEM], scratch, flops)(
        place, other, *near, *far, first
    )
    pieces = lax.all_to_all(pieces, ("q", "c", "z"), 0, 0, tiled=True)
    return kernel(sum_kernel, PIECE, [SMEM, SMEM, VMEM])(block_order, place, pieces)


def solution(mesh):
    grid = Mesh(mesh.devices.reshape(NX, NF, NQ, NC, NZ), AXES)
    spec = P(None, AXES[:4], "z")
    return jax.shard_map(
        local, mesh=grid, in_specs=(spec,) * 4 + (P(),), out_specs=spec, check_vma=False
    )
```

```python
import jax
import jax.numpy as jnp
from jax import lax
from jax.experimental import pallas as pl
from jax.experimental.pallas import tpu as pltpu
from jax.sharding import Mesh, PartitionSpec as P

NX, NF, NQ, NC, NZ = 4, 2, 4, 2, 8
AXES = ("x", "f", "q", "c", "z")
NH, ROWS, DEPTH = 3, 48, 384
BLOCK = (2, NH, ROWS, DEPTH)
PIECE = (NH, ROWS, DEPTH)
NP = NQ * NC
LANES = 128
LAST = 2 * ROWS
KEPT = LANES - LAST
LEFT = ROWS - KEPT
GROUP = 8
PACKED = (ROWS + GROUP, LANES)
VMEM = pl.BlockSpec(memory_space=pltpu.VMEM)
ANY = pl.BlockSpec(memory_space=pl.ANY)
SMEM = pl.BlockSpec(memory_space=pltpu.SMEM)
PARAMS = pltpu.CompilerParams(vmem_limit_bytes=32 * 2**20)
BF16 = jnp.bfloat16


def left_kernel(amp, cross, out):
    for q in range(NQ):
        out[q, 0] = amp[...]
        out[q, 1] = cross[...]


def copy_kernel(src, *rest):
    rest[-1][...] = src[...]


def mask_kernel(order, place, rows, *rest):
    out = rest[-1]
    k = place[4] * DEPTH + lax.broadcasted_iota(jnp.int32, (1, DEPTH), 1)
    for h in range(NH):
        live = k < order[h]
        for q in range(NQ):
            for pair in range(2):
                block = rows[q, pair, h]
                out[pair, h, q] = jnp.where(live, block, jnp.zeros_like(block))


def tile_kernel(place, own, other, *rest):
    near, far, (out, rhs) = rest[:NX], rest[NX : 2 * NX], rest[2 * NX :]
    x0, f, c = place[0], place[1], place[3]
    for x in range(NX):
        for h in range(NH):
            for pair in range(2):
                rhs[h, pair, 2 * lax.rem(x0 + x, NX) + f] = near[x][pair, h]
                rhs[h, pair, 2 * lax.rem(x0 + x, NX) + 1 - f] = far[x][pair, h]
    for side, rows in enumerate((own, other)):
        core = lax.rem(c + side, NC)
        totals = []
        for h in range(NH):
            total = None
            for pair in range(2):
                part = lax.dot_general(
                    rows[pair, h].reshape(NQ * ROWS, DEPTH),
                    rhs[h, pair].reshape(NZ * ROWS, DEPTH),
                    (((1,), (1,)), ((), ())),
                    preferred_element_type=jnp.float32,
                )
                total = part if total is None else total + part
            totals.append(total)
        pack(totals, out, core)


def pack(totals, out, core):
    fill = jnp.zeros((GROUP, LANES - ROWS // GROUP * LEFT), jnp.float32)
    for q in range(NQ):
        part = [t[q * ROWS : (q + 1) * ROWS] for t in totals]
        for z in range(NZ):
            at = z * ROWS
            main = jnp.concatenate(
                [part[0][:, at : at + ROWS], part[1][:, at : at + ROWS], part[2][:, at : at + KEPT]], axis=1
            )
            rest = part[2][:, at + KEPT : at + ROWS]
            rest = [rest[g : g + GROUP] for g in range(0, ROWS, GROUP)]
            rest = jnp.concatenate(rest + [fill], axis=1)
            out[(q * NC + core) * NZ + z] = jnp.concatenate([main, rest], axis=0).astype(BF16)


def sum_kernel(order, place, pieces, out):
    x, f, q, c, z = (place[i] for i in range(5))
    straight = lax.rem(z, 2) == f
    sums = []
    for s in range(NP):
        total = pieces[s * NZ].astype(jnp.float32)
        for r in range(1, NZ):
            total = total + pieces[s * NZ + r].astype(jnp.float32)
        sums.append(total)
    b = z * DEPTH + lax.broadcasted_iota(jnp.int32, (1, DEPTH), 1)
    a = (((x * NF + f) * NQ + q) * NC + c) * ROWS + lax.broadcasted_iota(jnp.int32, (ROWS, 1), 0)
    blocks = [[] for _ in range(NH)]
    for s in range(NP):
        mirrored = (NQ - 1 - s // NC) * NC + s % NC
        total = jnp.where(straight, sums[s], sums[mirrored])
        rest = [total[ROWS:, g * LEFT : (g + 1) * LEFT] for g in range(ROWS // GROUP)]
        rest = jnp.concatenate(rest, axis=0)
        blocks[0].append(total[:ROWS, :ROWS])
        blocks[1].append(total[:ROWS, ROWS:LAST])
        blocks[2].append(jnp.concatenate([total[:ROWS, LAST:], rest], axis=1))
    for h in range(NH):
        live = (a < order[h]) & (b < order[h])
        whole = jnp.concatenate(blocks[h], axis=1)
        out[h] = jnp.where(live, whole, 0.0).astype(BF16)


def kernel(body, shapes, specs, scratch=(), flops=0):
    make = lambda shape: jax.ShapeDtypeStruct(shape, BF16)
    many = isinstance(shapes, list)
    return pl.pallas_call(
        body,
        out_shape=[make(shape) for shape in shapes] if many else make(shapes),
        in_specs=specs,
        out_specs=[VMEM] * len(shapes) if many else VMEM,
        scratch_shapes=[pltpu.VMEM(shape, BF16) for shape in scratch],
        compiler_params=PARAMS,
        cost_estimate=pl.CostEstimate(flops=flops, bytes_accessed=2**21, transcendentals=0),
    )


def local(amplitudes, crossed, coulomb, exchange_int, block_order):
    place = [lax.axis_index(n) for n in AXES]
    place = jnp.stack(place).astype(jnp.int32)

    def along_x(block):
        return [block] + [
            lax.ppermute(block, "x", [((i + e) % NX, i) for i in range(NX)]) for e in range(1, NX)
        ]

    right = jnp.stack([coulomb, exchange_int])
    n = NF * NQ
    mirror = lax.ppermute(right, ("f", "q"), [(i, n - 1 - i) for i in range(n)])
    near = along_x(right)
    left = kernel(left_kernel, (NQ,) + BLOCK, [VMEM] * 2)(amplitudes, crossed)
    own = lax.all_to_all(left, "q", 0, 0, tiled=True)
    mirror = kernel(copy_kernel, BLOCK, [VMEM, ANY], flops=10**10)(mirror, right)
    far = along_x(mirror)
    own = kernel(mask_kernel, (2, NH, NQ, ROWS, DEPTH), [SMEM, SMEM, VMEM, ANY])(
        block_order, place, own, right
    )
    other = lax.ppermute(own, "c", [(0, 1), (1, 0)])
    flops = 4 * NH * (NP * ROWS) ** 2 * DEPTH
    last = kernel(copy_kernel, BLOCK, [VMEM] + [ANY] * 5, flops=12 * 10**9)(
        far[3], far[1], far[2], *near[1:]
    )
    pieces = kernel(
        tile_kernel,
        (NP * NZ,) + PACKED,
        [SMEM] + [VMEM] * (2 + 2 * NX),
        [(NH, 2, NZ, ROWS, DEPTH)],
        flops,
    )(place, own, other, *near, *far[:3], last)
    pieces = lax.all_to_all(pieces, ("q", "c", "z"), 0, 0, tiled=True)
    return kernel(sum_kernel, PIECE, [SMEM, SMEM, VMEM])(block_order, place, pieces)


def solution(mesh):
    grid = Mesh(mesh.devices.reshape(NX, NF, NQ, NC, NZ), AXES)
    spec = P(None, AXES[:4], "z")
    return jax.shard_map(
        local, mesh=grid, in_specs=(spec,) * 4 + (P(),), out_specs=spec, check_vma=False
    )
```
